32 devices in a mesh: space: 8 (over y, x, core), view: 4 (over z).
Axes of the slice: x: 2, y: 2, z: 4, core: 2. Of those that a mesh axis runs over, the one named last changes fastest.
Arguments:
- estimate: float32 [512, 32, 256], P('space'), may hold values from 0.5 to 2
- images: bfloat16 [8, 512, 32, 256], P('view', 'space'), may hold values from 0.5 to 2
- kernel_halves: float32 [8, 3, 16], P('view'), may hold values from 0.02 to 1
Outputs:
- new_estimate: float32 [512, 32, 256], P('space', 'view')
The draws below stay inside these ranges and needn't reach their ends.
All inputs are finite; a program needn't handle non-finite values.
Results may differ from the reference program's by a relative error of at most 0.0003.
Values sent between devices are 32-bit elements; how exact they have to be, the bound alone decides.
A program may use at most 128 MiB of HBM per device.

```python
import math
import jax
import jax.numpy as jnp
from jax import lax

VIEWS = 8
HALF = 16
XPIX = 32
YPIX = 256
ITERS = 2
NZ = 512


def block_levels(key, dims, shards, smallest, high):
    def one(position, parts):
        heights = jax.random.uniform(jax.random.fold_in(jax.random.fold_in(key, 6), position), (parts,), jnp.float32, smallest / len(shards), high / len(shards))
        return jnp.repeat(jnp.exp(heights), dims[position] // parts).reshape((-1,) + (1,) * (len(dims) - position - 1))

    factor_of = one(*shards[0])
    for cut in shards[1:]:
        factor_of = factor_of * one(*cut)
    return factor_of


def setup_inputs(seed: int = 0) -> dict:
    keys = jax.random.split(jax.random.key(seed), 4)
    estimate = jnp.clip(jnp.exp(math.log(2.0) - 1.3862944 * jax.random.uniform(keys[0], (NZ, XPIX, YPIX), jnp.float32) ** block_levels(keys[0], (NZ, XPIX, YPIX), ((0, 8),), -0.2, 0.2)), 0.5, 2.0)
    images = jnp.clip(jnp.exp(math.log(2.0) - 1.3862944 * jax.random.uniform(keys[1], (VIEWS, NZ, XPIX, YPIX), jnp.float32) ** block_levels(keys[1], (VIEWS, NZ, XPIX, YPIX), ((0, 4), (1, 8)), -0.2, 0.2)), 0.5, 2.0).astype(jnp.bfloat16)
    kernel_halves = jnp.clip(jnp.exp(math.log(1.0) - 3.912023 * jax.random.uniform(keys[2], (VIEWS, 3, HALF), jnp.float32) ** block_levels(keys[2], (VIEWS, 3, HALF), ((0, 4),), -0.2, 0.2)), 0.02, 1.0)
    return {"estimate": estimate, "images": images, "kernel_halves": kernel_halves}


def normalize(kernel_halves):
    kernel_sum = kernel_halves[..., 0] + 2.0 * jnp.sum(kernel_halves[..., 1:], axis=-1)
    return kernel_halves / kernel_sum[..., None]


def smooth_axis(field, kernel_row, axis_number):
    radius = kernel_row.shape[0] - 1
    length = field.shape[axis_number]
    widths = [(0, 0), (0, 0), (0, 0)]
    widths[axis_number] = (radius, radius)
    padded = jnp.pad(field, widths)
    result = jnp.zeros(field.shape, jnp.float32)
    for offset in range(2 * radius + 1):
        weight = kernel_row[abs(offset - radius)]
        result = result + weight * lax.slice_in_dim(padded, offset, offset + length, axis=axis_number)
    return result


def blur(field, kernel_set):
    result = smooth_axis(field, kernel_set[2], 2)
    result = smooth_axis(result, kernel_set[1], 1)
    return smooth_axis(result, kernel_set[0], 0)


def reference(estimate, images, kernel_halves):
    kernels = normalize(kernel_halves)
    current = estimate
    for iteration in range(ITERS):
        def accumulate(product, inputs):
            picture, kernel_set = inputs
            blurred = blur(current, kernel_set)
            quotient = picture.astype(jnp.float32) / blurred
            return product * blur(quotient, kernel_set), None

        combined, unused = lax.scan(accumulate, jnp.ones(current.shape, jnp.float32), (images, kernels))
        current = current * combined
    return current
```

```python
import functools

import jax
import jax.numpy as jnp
from jax import lax
from jax.experimental import pallas as pl
from jax.experimental.pallas import tpu as pltpu
from jax.sharding import PartitionSpec as P

ITERS = 2
CHUNK = 8
MESH = pl.DeviceIdType.MESH

precise = lax.Precision.HIGH


def extended(array, dim, width):
    size, length = lax.axis_size("space"), array.shape[dim]
    up = [(i, i + 1) for i in range(size - 1)]
    down = [(j, i) for i, j in up]
    last = lax.slice_in_dim(array, length - width, length, axis=dim)
    leading = lax.slice_in_dim(array, 0, width, axis=dim)
    before = lax.ppermute(last, "space", up)
    after = lax.ppermute(leading, "space", down)
    return jnp.concatenate([before, array, after], axis=dim)


def normalize(kernel_halves):
    kernel_sum = kernel_halves[..., 0] + 2.0 * jnp.sum(kernel_halves[..., 1:], axis=-1)
    return kernel_halves / kernel_sum[..., None]


def band_matrix(kernel_row, row_count, col_count, offset):
    radius = kernel_row.shape[0] - 1
    distance = jnp.abs(
        jnp.arange(col_count, dtype=jnp.int32)[None, :]
        - jnp.arange(row_count, dtype=jnp.int32)[:, None]
        - offset
    )
    matrix = jnp.zeros((row_count, col_count), jnp.float32)
    for lag_value in range(radius + 1):
        matrix = matrix + jnp.where(distance == lag_value, kernel_row[lag_value], 0.0)
    return matrix


def cross_pass(along_y, cross_mats):
    return jnp.einsum("nvx,nzxy->nzvy", cross_mats, along_y, precision=precise)


def depth_pass(padded, depth_mats):
    return jnp.einsum("nab,nbxy->naxy", depth_mats, padded, precision=precise)


def merge_kernel(n, gather, f_ref, cur_ref, out_ref, from_left, from_right, *sems):
    recv_l, recv_r, send_r, send_l = sems[:4]
    me = lax.axis_index("view")
    chunks, rows = from_left.shape[1], from_left.shape[3]
    right = {"view": jnp.minimum(me + 1, n - 1)}
    left = {"view": jnp.maximum(me - 1, 0)}

    barrier = pltpu.get_barrier_semaphore()

    @pl.when(me > 0)
    def _():
        pl.semaphore_signal(barrier, inc=1, device_id=left, device_id_type=MESH)

    @pl.when(me < n - 1)
    def _():
        pl.semaphore_signal(barrier, inc=1, device_id=right, device_id_type=MESH)

    pl.semaphore_wait(barrier, (me > 0).astype(jnp.int32) + (me < n - 1).astype(jnp.int32))

    def right_copy(k, c):
        return pltpu.make_async_remote_copy(
            from_left.at[k, c], from_left.at[k, c], send_r.at[k, c], recv_l.at[k, c],
            device_id=right, device_id_type=MESH)

    def left_copy(k, c):
        return pltpu.make_async_remote_copy(
            from_right.at[k, c], from_right.at[k, c], send_l.at[k, c], recv_r.at[k, c],
            device_id=left, device_id_type=MESH)

    def place(k, c):
        return out_ref.at[pl.ds(c * CHUNK, CHUNK), pl.ds(k * rows, rows), :]

    def back_copy(k, c, goes_right):
        recv, to_right, to_left = sems[4:]
        return pltpu.make_async_remote_copy(
            place(k, c), place(k, c), (to_right if goes_right else to_left).at[k, c], recv.at[k, c],
            device_id=right if goes_right else left, device_id_type=MESH)

    def own(k, c):
        spot = (pl.ds(c * CHUNK, CHUNK), pl.ds(k * rows, rows))
        return f_ref[(0,) + spot] * f_ref[(1,) + spot]

    def step(s, carry):
        c_l = s - me
        for k in range(n - 1, 0, -1):
            @pl.when((k > me) & (c_l >= 0) & (c_l < chunks))
            def _():
                @pl.when(me == 0)
                def _():
                    from_left[k, c_l] = own(k, c_l)

                @pl.when(me > 0)
                def _():
                    right_copy(k, c_l).wait_recv()
                    from_left[k, c_l] = from_left[k, c_l] * own(k, c_l)

                right_copy(k, c_l).start()

        c_r = s - (n - 1 - me)
        for k in range(n - 1):
            @pl.when((k < me) & (c_r >= 0) & (c_r < chunks))
            def _():
                @pl.when(me == n - 1)
                def _():
                    from_right[k, c_r] = own(k, c_r)

                @pl.when(me < n - 1)
                def _():
                    left_copy(k, c_r).wait_recv()
                    from_right[k, c_r] = from_right[k, c_r] * own(k, c_r)

                left_copy(k, c_r).start()

        c_o = s - (n - 1)
        for k in range(n):
            @pl.when((k == me) & (c_o >= 0) & (c_o < chunks))
            def _():
                total = own(k, c_o)
                if k > 0:
                    right_copy(k, c_o).wait_recv()
                    total = total * from_left[k, c_o]
                if k < n - 1:
                    left_copy(k, c_o).wait_recv()
                    total = total * from_right[k, c_o]
                planes = pl.ds(c_o * CHUNK, CHUNK)
                segment = pl.ds(k * rows, rows)
                total = total * cur_ref[planes, segment, :]
                if gather:
                    out_ref[planes, segment, :] = total
                    if k > 0:
                        back_copy(k, c_o, False).start()
                    if k < n - 1:
                        back_copy(k, c_o, True).start()
                else:
                    out_ref[planes, :, :] = total

        if gather:
            for k in range(n):
                c_g = s - (n - 1) - jnp.abs(me - k)
                live = (c_g >= 0) & (c_g < chunks)

                @pl.when((k < me) & live)
                def _():
                    back_copy(k, c_g, True).wait_recv()

                    @pl.when(me < n - 1)
                    def _():
                        back_copy(k, c_g, True).start()

                @pl.when((k > me) & live)
                def _():
                    back_copy(k, c_g, False).wait_recv()

                    @pl.when(me > 0)
                    def _():
                        back_copy(k, c_g, False).start()

        return carry

    lax.fori_loop(0, chunks + (n - 1) * (2 if gather else 1), step, 0)

    def finish(c, carry):
        for k in range(n):
            @pl.when(k > me)
            def _():
                right_copy(k, c).wait_send()

            @pl.when(k < me)
            def _():
                left_copy(k, c).wait_send()

            if gather:
                @pl.when((k <= me) & (me < n - 1))
                def _():
                    back_copy(k, c, True).wait_send()

                @pl.when((k >= me) & (me > 0))
                def _():
                    back_copy(k, c, False).wait_send()

        return carry

    lax.fori_loop(0, chunks, finish, 0)


def merged(factors, current, gather):
    n = lax.axis_size("view")
    planes, width_x, width_y = current.shape
    rows, chunks = width_x // n, planes // CHUNK
    vmem = pl.BlockSpec(memory_space=pltpu.VMEM)
    land = pltpu.VMEM((n, chunks, CHUNK, rows, width_y), jnp.float32)
    return pl.pallas_call(
        functools.partial(merge_kernel, n, gather),
        out_shape=jax.ShapeDtypeStruct((planes, width_x if gather else rows, width_y), jnp.float32),
        in_specs=[vmem, vmem],
        out_specs=vmem,
        scratch_shapes=[land, land] + [pltpu.SemaphoreType.DMA((n, chunks))] * (7 if gather else 4),
        compiler_params=pltpu.CompilerParams(
            collective_id=1 if gather else 2, has_side_effects=True, vmem_limit_bytes=32 << 20),
    )(factors, current)


def on_device(estimate, images, kernel_halves):
    planes, width_x, width_y = estimate.shape
    kernels = normalize(kernel_halves)
    radius = kernels.shape[2] - 1
    depth_mats = jax.vmap(
        lambda kernel_row: band_matrix(kernel_row, planes, planes + 2 * radius, radius)
    )(kernels[:, 0])
    cross_mats = jax.vmap(lambda kernel_row: band_matrix(kernel_row, width_x, width_x, 0))(
        kernels[:, 1]
    )
    lateral_mats = jax.vmap(lambda kernel_row: band_matrix(kernel_row, width_y, width_y, 0))(
        kernels[:, 2]
    )
    pictures = images.astype(jnp.float32)
    current = estimate
    for iteration in range(ITERS):
        padded = extended(current, 0, radius)
        along_y = jnp.einsum("zxy,nyw->nzxw", padded, lateral_mats, precision=precise)
        blurred = depth_pass(cross_pass(along_y, cross_mats), depth_mats)
        quotients = pictures / blurred
        smoothed = cross_pass(
            jnp.einsum("nzxy,nyw->nzxw", quotients, lateral_mats, precision=precise), cross_mats
        )
        factors = depth_pass(extended(smoothed, 1, radius), depth_mats)
        current = merged(factors, current, iteration < ITERS - 1)
    return current


def solution(mesh):
    placed = (P("space", None, None), P("view", "space", None, None), P("view", None, None))
    return jax.shard_map(
        on_device, mesh=mesh, in_specs=placed, out_specs=P("space", "view", None), check_vma=False
    )
```

```python
import functools

import jax
import jax.numpy as jnp
from jax import lax
from jax.experimental import pallas as pl
from jax.experimental.pallas import tpu as pltpu
from jax.sharding import PartitionSpec as P

ITERS = 2
CHUNK = 4
MESH = pl.DeviceIdType.MESH

precise = lax.Precision.HIGH


def extended(array, dim, width):
    size, length = lax.axis_size("space"), array.shape[dim]
    up = [(i, i + 1) for i in range(size - 1)]
    down = [(j, i) for i, j in up]
    last = lax.slice_in_dim(array, length - width, length, axis=dim)
    leading = lax.slice_in_dim(array, 0, width, axis=dim)
    before = lax.ppermute(last, "space", up)
    after = lax.ppermute(leading, "space", down)
    return jnp.concatenate([before, array, after], axis=dim)


def normalize(kernel_halves):
    kernel_sum = kernel_halves[..., 0] + 2.0 * jnp.sum(kernel_halves[..., 1:], axis=-1)
    return kernel_halves / kernel_sum[..., None]


def band_matrix(kernel_row, row_count, col_count, offset):
    radius = kernel_row.shape[0] - 1
    distance = jnp.abs(
        jnp.arange(col_count, dtype=jnp.int32)[None, :]
        - jnp.arange(row_count, dtype=jnp.int32)[:, None]
        - offset
    )
    matrix = jnp.zeros((row_count, col_count), jnp.float32)
    for lag_value in range(radius + 1):
        matrix = matrix + jnp.where(distance == lag_value, kernel_row[lag_value], 0.0)
    return matrix


def cross_pass(along_y, cross_mats):
    return jnp.einsum("nvx,nzxy->nzvy", cross_mats, along_y, precision=precise)


def depth_pass(padded, depth_mats):
    return jnp.einsum("nab,nbxy->naxy", depth_mats, padded, precision=precise)


def merge_kernel(n, gather, f_ref, cur_ref, out_ref, from_left, from_right, *sems):
    recv_l, recv_r, send_r, send_l = sems[:4]
    me = lax.axis_index("view")
    chunks, rows = from_left.shape[1], from_left.shape[3]
    right = {"view": jnp.minimum(me + 1, n - 1)}
    left = {"view": jnp.maximum(me - 1, 0)}

    barrier = pltpu.get_barrier_semaphore()

    @pl.when(me > 0)
    def _():
        pl.semaphore_signal(barrier, inc=1, device_id=left, device_id_type=MESH)

    @pl.when(me < n - 1)
    def _():
        pl.semaphore_signal(barrier, inc=1, device_id=right, device_id_type=MESH)

    pl.semaphore_wait(barrier, (me > 0).astype(jnp.int32) + (me < n - 1).astype(jnp.int32))

    def right_copy(k, c):
        return pltpu.make_async_remote_copy(
            from_left.at[k, c], from_left.at[k, c], send_r.at[k, c], recv_l.at[k, c],
            device_id=right, device_id_type=MESH)

    def left_copy(k, c):
        return pltpu.make_async_remote_copy(
            from_right.at[k, c], from_right.at[k, c], send_l.at[k, c], recv_r.at[k, c],
            device_id=left, device_id_type=MESH)

    def place(k, c):
        return out_ref.at[pl.ds(c * CHUNK, CHUNK), pl.ds(k * rows, rows), :]

    def back_copy(k, c, goes_right):
        recv, to_right, to_left = sems[4:]
        return pltpu.make_async_remote_copy(
            place(k, c), place(k, c), (to_right if goes_right else to_left).at[k, c], recv.at[k, c],
            device_id=right if goes_right else left, device_id_type=MESH)

    def own(k, c):
        spot = (pl.ds(c * CHUNK, CHUNK), pl.ds(k * rows, rows))
        return f_ref[(0,) + spot] * f_ref[(1,) + spot]

    def step(s, carry):
        c_l = s - me
        for k in range(n - 1, 0, -1):
            @pl.when((k > me) & (c_l >= 0) & (c_l < chunks))
            def _():
                @pl.when(me == 0)
                def _():
                    from_left[k, c_l] = own(k, c_l)

                @pl.when(me > 0)
                def _():
                    right_copy(k, c_l).wait_recv()
                    from_left[k, c_l] = from_left[k, c_l] * own(k, c_l)

                right_copy(k, c_l).start()

        c_r = s - (n - 1 - me)
        for k in range(n - 1):
            @pl.when((k < me) & (c_r >= 0) & (c_r < chunks))
            def _():
                @pl.when(me == n - 1)
                def _():
                    from_right[k, c_r] = own(k, c_r)

                @pl.when(me < n - 1)
                def _():
                    left_copy(k, c_r).wait_recv()
                    from_right[k, c_r] = from_right[k, c_r] * own(k, c_r)

                left_copy(k, c_r).start()

        c_o = s - (n - 1)
        for k in range(n):
            @pl.when((k == me) & (c_o >= 0) & (c_o < chunks))
            def _():
                total = own(k, c_o)
                if k > 0:
                    right_copy(k, c_o).wait_recv()
                    total = total * from_left[k, c_o]
                if k < n - 1:
                    left_copy(k, c_o).wait_recv()
                    total = total * from_right[k, c_o]
                planes = pl.ds(c_o * CHUNK, CHUNK)
                segment = pl.ds(k * rows, rows)
                total = total * cur_ref[planes, segment, :]
                if gather:
                    out_ref[planes, segment, :] = total
                    if k > 0:
                        back_copy(k, c_o, False).start()
                    if k < n - 1:
                        back_copy(k, c_o, True).start()
                else:
                    out_ref[planes, :, :] = total

        if gather:
            for k in range(n):
                c_g = s - (n - 1) - jnp.abs(me - k)
                live = (c_g >= 0) & (c_g < chunks)

                @pl.when((k < me) & live)
                def _():
                    back_copy(k, c_g, True).wait_recv()

                    @pl.when(me < n - 1)
                    def _():
                        back_copy(k, c_g, True).start()

                @pl.when((k > me) & live)
                def _():
                    back_copy(k, c_g, False).wait_recv()

                    @pl.when(me > 0)
                    def _():
                        back_copy(k, c_g, False).start()

        return carry

    lax.fori_loop(0, chunks + (n - 1) * (2 if gather else 1), step, 0)

    def finish(c, carry):
        for k in range(n):
            @pl.when(k > me)
            def _():
                right_copy(k, c).wait_send()

            @pl.when(k < me)
            def _():
                left_copy(k, c).wait_send()

            if gather:
                @pl.when((k <= me) & (me < n - 1))
                def _():
                    back_copy(k, c, True).wait_send()

                @pl.when((k >= me) & (me > 0))
                def _():
                    back_copy(k, c, False).wait_send()

        return carry

    lax.fori_loop(0, chunks, finish, 0)


def merged(factors, current, gather):
    n = lax.axis_size("view")
    planes, width_x, width_y = current.shape
    rows, chunks = width_x // n, planes // CHUNK
    vmem = pl.BlockSpec(memory_space=pltpu.VMEM)
    land = pltpu.VMEM((n, chunks, CHUNK, rows, width_y), jnp.float32)
    return pl.pallas_call(
        functools.partial(merge_kernel, n, gather),
        out_shape=jax.ShapeDtypeStruct((planes, width_x if gather else rows, width_y), jnp.float32),
        in_specs=[vmem, vmem],
        out_specs=vmem,
        scratch_shapes=[land, land] + [pltpu.SemaphoreType.DMA((n, chunks))] * (7 if gather else 4),
        compiler_params=pltpu.CompilerParams(
            collective_id=1 if gather else 2, has_side_effects=True, vmem_limit_bytes=32 << 20),
    )(factors, current)


def on_device(estimate, images, kernel_halves):
    planes, width_x, width_y = estimate.shape
    kernels = normalize(kernel_halves)
    radius = kernels.shape[2] - 1
    depth_mats = jax.vmap(
        lambda kernel_row: band_matrix(kernel_row, planes, planes + 2 * radius, radius)
    )(kernels[:, 0])
    cross_mats = jax.vmap(lambda kernel_row: band_matrix(kernel_row, width_x, width_x, 0))(
        kernels[:, 1]
    )
    lateral_mats = jax.vmap(lambda kernel_row: band_matrix(kernel_row, width_y, width_y, 0))(
        kernels[:, 2]
    )
    pictures = images.astype(jnp.float32)
    current = estimate
    for iteration in range(ITERS):
        padded = extended(current, 0, radius)
        along_y = jnp.einsum("zxy,nyw->nzxw", padded, lateral_mats, precision=precise)
        blurred = depth_pass(cross_pass(along_y, cross_mats), depth_mats)
        quotients = pictures / blurred
        smoothed = cross_pass(
            jnp.einsum("nzxy,nyw->nzxw", quotients, lateral_mats, precision=precise), cross_mats
        )
        factors = depth_pass(extended(smoothed, 1, radius), depth_mats)
        current = merged(factors, current, iteration < ITERS - 1)
    return current


def solution(mesh):
    placed = (P("space", None, None), P("view", "space", None, None), P("view", None, None))
    return jax.shard_map(
        on_device, mesh=mesh, in_specs=placed, out_specs=P("space", "view", None), check_vma=False
    )
```

```python
import functools

import jax
import jax.numpy as jnp
from jax import lax
from jax.experimental import pallas as pl
from jax.experimental.pallas import tpu as pltpu
from jax.sharding import PartitionSpec as P

ITERS = 2
CHUNK = 8
MESH = pl.DeviceIdType.MESH

precise = lax.Precision.HIGH


def extended(array, dim, width):
    size, length = lax.axis_size("space"), array.shape[dim]
    up = [(i, i + 1) for i in range(size - 1)]
    down = [(j, i) for i, j in up]
    last = lax.slice_in_dim(array, length - width, length, axis=dim)
    leading = lax.slice_in_dim(array, 0, width, axis=dim)
    before = lax.ppermute(last, "space", up)
    after = lax.ppermute(leading, "space", down)
    return jnp.concatenate([before, array, after], axis=dim)


def mats_kernel(halves_ref, depth_ref, cross_ref, lateral_ref):
    views, _, taps = halves_ref.shape
    for a, (out_ref, offset) in enumerate(((depth_ref, taps - 1), (cross_ref, 0), (lateral_ref, 0))):
        row_count, col_count = out_ref.shape[1:]
        block = min(row_count, 32)
        shape = (block, col_count)
        lag = lax.broadcasted_iota(jnp.int32, shape, 1) - lax.broadcasted_iota(jnp.int32, shape, 0)
        for v in range(views):
            side = halves_ref[v, a, 1]
            for j in range(2, taps):
                side = side + halves_ref[v, a, j]
            kernel_sum = jnp.full(shape, halves_ref[v, a, 0] + 2.0 * side)
            for first in range(0, row_count, block):
                distance = jnp.abs(lag - (offset + first))
                matrix = jnp.zeros(shape, jnp.float32)
                for j in range(taps):
                    matrix = jnp.where(distance == j, halves_ref[v, a, j], matrix)
                out_ref[v, first:first + block, :] = matrix / kernel_sum


def band_matrices(kernel_halves, planes, width_x, width_y):
    views, _, taps = kernel_halves.shape
    shapes = ((planes, planes + 2 * (taps - 1)), (width_x, width_x), (width_y, width_y))
    return pl.pallas_call(
        mats_kernel,
        out_shape=[jax.ShapeDtypeStruct((views,) + shape, jnp.float32) for shape in shapes],
        in_specs=[pl.BlockSpec(memory_space=pltpu.SMEM)],
        out_specs=[pl.BlockSpec(memory_space=pltpu.VMEM)] * 3,
        cost_estimate=pl.CostEstimate(flops=8 << 20, bytes_accessed=1 << 20, transcendentals=0),
    )(kernel_halves)


def cross_pass(along_y, cross_mats):
    return jnp.einsum("nvx,nzxy->nzvy", cross_mats, along_y, precision=precise)


def depth_pass(padded, depth_mats):
    return jnp.einsum("nab,nbxy->naxy", depth_mats, padded, precision=precise)


def merge_kernel(n, gather, f_ref, cur_ref, out_ref, from_left, from_right, *sems):
    recv_l, recv_r, send_r, send_l = sems[:4]
    me = lax.axis_index("view")
    chunks, rows = from_left.shape[1], from_left.shape[3]
    right = {"view": jnp.minimum(me + 1, n - 1)}
    left = {"view": jnp.maximum(me - 1, 0)}

    barrier = pltpu.get_barrier_semaphore()

    @pl.when(me > 0)
    def _():
        pl.semaphore_signal(barrier, inc=1, device_id=left, device_id_type=MESH)

    @pl.when(me < n - 1)
    def _():
        pl.semaphore_signal(barrier, inc=1, device_id=right, device_id_type=MESH)

    pl.semaphore_wait(barrier, (me > 0).astype(jnp.int32) + (me < n - 1).astype(jnp.int32))

    def right_copy(k, c):
        return pltpu.make_async_remote_copy(
            from_left.at[k, c], from_left.at[k, c], send_r.at[k, c], recv_l.at[k, c],
            device_id=right, device_id_type=MESH)

    def left_copy(k, c):
        return pltpu.make_async_remote_copy(
            from_right.at[k, c], from_right.at[k, c], send_l.at[k, c], recv_r.at[k, c],
            device_id=left, device_id_type=MESH)

    def place(k, c):
        return out_ref.at[pl.ds(c * CHUNK, CHUNK), pl.ds(k * rows, rows), :]

    def back_copy(k, c, goes_right):
        recv, to_right, to_left = sems[4:]
        return pltpu.make_async_remote_copy(
            place(k, c), place(k, c), (to_right if goes_right else to_left).at[k, c], recv.at[k, c],
            device_id=right if goes_right else left, device_id_type=MESH)

    def own(k, c):
        spot = (pl.ds(c * CHUNK, CHUNK), pl.ds(k * rows, rows))
        return f_ref[(0,) + spot] * f_ref[(1,) + spot]

    def step(s, carry):
        c_l = s - me
        for k in range(n - 1, 0, -1):
            @pl.when((k > me) & (c_l >= 0) & (c_l < chunks))
            def _():
                @pl.when(me == 0)
                def _():
                    from_left[k, c_l] = own(k, c_l)

                @pl.when(me > 0)
                def _():
                    right_copy(k, c_l).wait_recv()
                    from_left[k, c_l] = from_left[k, c_l] * own(k, c_l)

                right_copy(k, c_l).start()

        c_r = s - (n - 1 - me)
        for k in range(n - 1):
            @pl.when((k < me) & (c_r >= 0) & (c_r < chunks))
            def _():
                @pl.when(me == n - 1)
                def _():
                    from_right[k, c_r] = own(k, c_r)

                @pl.when(me < n - 1)
                def _():
                    left_copy(k, c_r).wait_recv()
                    from_right[k, c_r] = from_right[k, c_r] * own(k, c_r)

                left_copy(k, c_r).start()

        c_o = s - (n - 1)
        for k in range(n):
            @pl.when((k == me) & (c_o >= 0) & (c_o < chunks))
            def _():
                total = own(k, c_o)
                if k > 0:
                    right_copy(k, c_o).wait_recv()
                    total = total * from_left[k, c_o]
                if k < n - 1:
                    left_copy(k, c_o).wait_recv()
                    total = total * from_right[k, c_o]
                planes = pl.ds(c_o * CHUNK, CHUNK)
                segment = pl.ds(k * rows, rows)
                total = total * cur_ref[planes, segment, :]
                if gather:
                    out_ref[planes, segment, :] = total
                    if k > 0:
                        back_copy(k, c_o, False).start()
                    if k < n - 1:
                        back_copy(k, c_o, True).start()
                else:
                    out_ref[planes, :, :] = total

        if gather:
            for k in range(n):
                c_g = s - (n - 1) - jnp.abs(me - k)
                live = (c_g >= 0) & (c_g < chunks)

                @pl.when((k < me) & live)
                def _():
                    back_copy(k, c_g, True).wait_recv()

                    @pl.when(me < n - 1)
                    def _():
                        back_copy(k, c_g, True).start()

                @pl.when((k > me) & live)
                def _():
                    back_copy(k, c_g, False).wait_recv()

                    @pl.when(me > 0)
                    def _():
                        back_copy(k, c_g, False).start()

        return carry

    lax.fori_loop(0, chunks + (n - 1) * (2 if gather else 1), step, 0)

    def finish(c, carry):
        for k in range(n):
            @pl.when(k > me)
            def _():
                right_copy(k, c).wait_send()

            @pl.when(k < me)
            def _():
                left_copy(k, c).wait_send()

            if gather:
                @pl.when((k <= me) & (me < n - 1))
                def _():
                    back_copy(k, c, True).wait_send()

                @pl.when((k >= me) & (me > 0))
                def _():
                    back_copy(k, c, False).wait_send()

        return carry

    lax.fori_loop(0, chunks, finish, 0)


def merged(factors, current, gather):
    n = lax.axis_size("view")
    planes, width_x, width_y = current.shape
    rows, chunks = width_x // n, planes // CHUNK
    vmem = pl.BlockSpec(memory_space=pltpu.VMEM)
    land = pltpu.VMEM((n, chunks, CHUNK, rows, width_y), jnp.float32)
    return pl.pallas_call(
        functools.partial(merge_kernel, n, gather),
        out_shape=jax.ShapeDtypeStruct((planes, width_x if gather else rows, width_y), jnp.float32),
        in_specs=[vmem, vmem],
        out_specs=vmem,
        scratch_shapes=[land, land] + [pltpu.SemaphoreType.DMA((n, chunks))] * (7 if gather else 4),
        compiler_params=pltpu.CompilerParams(
            collective_id=1 if gather else 2, has_side_effects=True, vmem_limit_bytes=32 << 20),
    )(factors, current)


def on_device(estimate, images, kernel_halves):
    planes, width_x, width_y = estimate.shape
    radius = kernel_halves.shape[2] - 1
    depth_mats, cross_mats, lateral_mats = band_matrices(kernel_halves, planes, width_x, width_y)
    pictures = images.astype(jnp.float32)
    current = estimate
    for iteration in range(ITERS):
        padded = extended(current, 0, radius)
        along_y = jnp.einsum("zxy,nyw->nzxw", padded, lateral_mats, precision=precise)
        blurred = depth_pass(cross_pass(along_y, cross_mats), depth_mats)
        quotients = pictures / blurred
        smoothed = cross_pass(
            jnp.einsum("nzxy,nyw->nzxw", quotients, lateral_mats, precision=precise), cross_mats
        )
        factors = depth_pass(extended(smoothed, 1, radius), depth_mats)
        current = merged(factors, current, iteration < ITERS - 1)
    return current


def solution(mesh):
    placed = (P("space", None, None), P("view", "space", None, None), P("view", None, None))
    return jax.shard_map(
        on_device, mesh=mesh, in_specs=placed, out_specs=P("space", "view", None), check_vma=False
    )
```
